512 devices in a mesh: dp: 32 (over z_lo, x, core), mp: 16 (over z_hi, y).
Axes of the slice: x: 4, y: 8, z: 8 (z_hi: 2, z_lo: 4; z = z_hi * 4 + z_lo), core: 2. Of those that a mesh axis runs over, the one named last changes fastest.
Arguments:
- features: bfloat16 [4096, 8192], P('dp', 'mp'), may hold values from -110 to 110
- output_grads: bfloat16 [4096, 14336], P('dp', 'mp'), may hold values from -110 to 110
- basis: bfloat16 [8192, 512], P('dp'), may hold values from -0.0625 to 0.0625
- moment_one: float32 [8192, 14336], P('dp', 'mp'), may hold values from -4 to 4
- moment_two: float32 [8192, 14336], P('dp', 'mp'), may hold values from 0.02 to 0.5
Outputs:
- new_moment_one: float32 [8192, 14336], P('dp', 'mp')
- new_moment_two: float32 [8192, 14336], P('dp', 'mp')
- update: bfloat16 [8192, 14336], P('dp', 'mp')
The draws below stay inside these ranges and needn't reach their ends.
All inputs are finite; a program needn't handle non-finite values.
Results may differ from the reference program's by a relative error of at most 0.001.
Values may be sent and summed in bfloat16 or wider, within the bound.
No kernel may reach another device: no remote copies, remote signals or barrier semaphores. Data moves between devices by JAX's collectives and lax.ppermute only.
A program may use at most 64 MiB of HBM per device.

```python
import math
import jax
import jax.numpy as jnp
from jax import lax

D = 8192
FF = 14336
K = 512
TOKENS = 4096


def scaled_rows(key, rows, width, power):
    key_scale = jax.random.fold_in(key, 1)
    key_base = jax.random.fold_in(key, 2)
    scales = jnp.exp(jax.random.uniform(key_scale, (width,), jnp.float32) * 2.302585)
    ramp = (1.0 + 2.0 * jnp.arange(width, dtype=jnp.float32) / width) ** power
    base = jnp.clip(jax.random.normal(key_base, (rows, width), jnp.float32), -6.0, 6.0)
    return base * scales * ramp


def draw_features(key, part):
    key = jax.random.fold_in(key, 11)
    values = scaled_rows(key, TOKENS, D, 0.5)
    return values.astype(jnp.bfloat16)


def draw_output_grads(key, part):
    key = jax.random.fold_in(key, 23)
    values = scaled_rows(key, TOKENS, FF, 0.5)
    return values.astype(jnp.bfloat16)


def block_levels(key, extent, split, smallest, high):
    def one(position, parts):
        steps = jax.random.uniform(jax.random.fold_in(jax.random.fold_in(key, 6), position), (parts,), jnp.float32, smallest / len(split), high / len(split))
        return jnp.repeat(jnp.exp(steps), extent[position] // parts).reshape((-1,) + (1,) * (len(extent) - position - 1))

    level = one(*split[0])
    for cut in split[1:]:
        level = level * one(*cut)
    return level


def centred(own_key, shape, scale, bound, shards=(), kind=jnp.bfloat16):
    values = scale * jax.random.normal(own_key, shape, jnp.float32)
    if shards:
        values = values * block_levels(own_key, shape, shards, -0.22, 0.18)
    return jnp.clip(values, -bound, bound).astype(kind)


def setup_inputs(seed: int = 0) -> dict:
    key_list = jax.random.split(jax.random.key(seed), 6)
    return {
        "features": draw_features(jax.random.fold_in(key_list[5], 71), 0),
        "output_grads": draw_output_grads(jax.random.fold_in(key_list[5], 71), 0),
        "basis": centred(key_list[2], (D, K), D ** -0.5, 0.0625, ((0, 32),)),
        "moment_one": centred(key_list[3], (D, FF), 0.3, 4.0, ((0, 32), (1, 16)), jnp.float32),
        "moment_two": jnp.clip(jnp.exp(math.log(0.5) - 3.218876 * jax.random.uniform(key_list[4], (D, FF), jnp.float32) ** block_levels(key_list[4], (D, FF), ((0, 32), (1, 16)), -0.2, 0.2)), 0.02, 0.5),
    }


def reference(features, output_grads, basis, moment_one, moment_two):
    grad = jnp.dot(features.T, output_grads, preferred_element_type=jnp.float32)
    basis_f = basis.astype(jnp.float32)
    coeffs = jnp.dot(basis_f.T, grad, precision=lax.Precision.HIGHEST)
    projected = grad - jnp.dot(basis_f, coeffs, precision=lax.Precision.HIGHEST)
    mean_square = jnp.sum(projected * projected) / (D * FF)
    factor = jnp.minimum(1.0, lax.rsqrt(mean_square + 1e-06))
    clipped = factor * projected
    new_one = 0.9 * moment_one + 0.1 * clipped
    new_two = 0.95 * moment_two + 0.05 * clipped * clipped
    update = (new_one / (jnp.sqrt(new_two) + 1e-08)).astype(jnp.bfloat16)
    return (new_one, new_two, update)
```

```python
import jax
import jax.numpy as jnp
from jax import lax
from jax.experimental import pallas as pl
from jax.experimental.pallas import tpu as pltpu
from jax.sharding import Mesh, PartitionSpec as P

D = 8192
FF = 14336
ZL, X, C, ZH, Y = 4, 4, 2, 2, 8
AXES = ("zl", "x", "c", "zh", "y")
DP = ("zl", "x", "c")
MP = ("zh", "y")
Q = ("zl", "x")
f32 = jnp.float32
bf16 = jnp.bfloat16


def move(value, to):
    def index(zl, x, c, zh, y):
        return (((zl * X + x) * C + c) * ZH + zh) * Y + y

    pairs = [
        (index(zl, x, c, zh, y), index(*to(zl, x, c, zh, y)))
        for zl in range(ZL)
        for x in range(X)
        for c in range(C)
        for zh in range(ZH)
        for y in range(Y)
    ]
    return lax.ppermute(value, AXES, pairs)


def transpose_place(zl, x, c, zh, y):
    q, j = X * zl + x, Y * zh + y
    return j // X, j % X, c, q // Y, q % Y


def along_y(value, step):
    return move(value, lambda zl, x, c, zh, y: (zl, x, c, zh, (y + step) % Y))


def other_core(value):
    return move(value, lambda zl, x, c, zh, y: (zl, x, 1 - c, zh, y))


def other_half(value):
    return move(value, lambda zl, x, c, zh, y: (zl, x, c, 1 - zh, y))


def spread(value, axes, n):
    copies = jnp.broadcast_to(value[None], (n,) + value.shape)
    return lax.all_to_all(copies, axes, 0, 0, tiled=True)


def parts(value, n):
    out = []
    for _ in range(n - 1):
        top = lax.reduce_precision(value, 8, 7)
        out.append(top.astype(bf16))
        value = value - top
    return out + [value.astype(bf16)]


def grad_kernel(place, g_ref, *refs):
    blocks, halves, (mine, theirs) = refs[:7], refs[7:9], refs[9:]
    y, c = place[0], place[1]
    for out, core in ((theirs, 1 - c), (mine, c)):
        rows = pl.ds(pl.multiple_of(core * 256, 256), 256)
        total = None
        for k, step in enumerate((0, -1, -2, -3, 1, 2, 3, 4)):
            at = lax.rem(y + (step + Y), Y)
            g = jnp.concatenate([g_ref[0, at], g_ref[1, at]], axis=0)
            if k < 7:
                high, low = blocks[k][rows, :256], blocks[k][rows, 256:]
            else:
                high, low = halves[0][rows, :], halves[1][rows, :]
            term = jnp.dot(high, g, preferred_element_type=f32)
            term += jnp.dot(low, g, preferred_element_type=f32)
            total = term if total is None else total + term
        out[...] = total


def on_device(features, output_grads, basis, moment_one, moment_two):
    c, zh, y = lax.axis_index("c"), lax.axis_index("zh"), lax.axis_index("y")
    cotangents = lax.all_gather(output_grads, Q, axis=0, tiled=True)

    own = move(features, transpose_place)
    basis_rows = lax.all_gather(basis, "c", axis=0, tiled=True)
    far = other_half(own)
    both = jnp.concatenate([jnp.where(zh == 0, own, far), jnp.where(zh == 0, far, own)])
    both = both.T.astype(f32)

    partial = jnp.dot(own, basis_rows, preferred_element_type=f32)
    pieces = lax.all_to_all(partial.reshape(16, 8, 512), Q, 0, 0, tiled=True)
    coded = spread(jnp.sum(pieces, axis=0), ("zh",) + Q, 32).reshape(256, 512)
    away = sum(
        lax.dot_general(
            basis_rows, p, (((1,), (1,)), ((), ())), preferred_element_type=f32
        )
        for p in parts(coded, 3)
    )
    kept = jnp.concatenate(parts(both - away, 2), axis=1)

    right, left = [kept], [kept]
    for _ in range(3):
        right.append(along_y(right[-1], 1))
        left.append(along_y(left[-1], -1))
    high = along_y(right[-1][:, :256], 1)
    low = along_y(left[-1][:, 256:], -1)

    tile = jax.ShapeDtypeStruct((256, 896), f32)
    vmem = pl.BlockSpec(memory_space=pltpu.VMEM)
    mine, theirs = pl.pallas_call(
        grad_kernel,
        out_shape=(tile, tile),
        in_specs=[pl.BlockSpec(memory_space=pltpu.SMEM)] + [vmem] * 10,
        out_specs=(vmem, vmem),
        compiler_params=pltpu.CompilerParams(vmem_limit_bytes=48 * 2**20),
        cost_estimate=pl.CostEstimate(
            flops=4 * 4096 * 256 * 896, bytes_accessed=10 * 2**20, transcendentals=0
        ),
    )(
        jnp.stack([y, c]).astype(jnp.int32),
        cotangents.reshape(ZH, Y, 128, 896),
        *right,
        *left[1:],
        high,
        low,
    )
    projected = mine + other_core(theirs)

    squares = jnp.sum((projected * projected).reshape(32, 8, 7, 128), axis=(0, 2))
    squares = jnp.sum(spread(squares, DP, 32), axis=0)
    square_sum = jnp.sum(spread(squares, MP, 16))
    mean_square = square_sum / (D * FF)
    factor = jnp.minimum(1.0, lax.rsqrt(mean_square + 1e-06))
    clipped = factor * projected
    new_one = 0.9 * moment_one + 0.1 * clipped
    new_two = 0.95 * moment_two + 0.05 * clipped * clipped
    update = (new_one / (jnp.sqrt(new_two) + 1e-08)).astype(bf16)
    return (new_one, new_two, update)


def solution(mesh):
    fine = Mesh(mesh.devices.reshape(ZL, X, C, ZH, Y), AXES)
    tile = P(DP, MP)
    return jax.shard_map(
        on_device,
        mesh=fine,
        in_specs=(tile, tile, P(DP, None), tile, tile),
        out_specs=(tile, tile, tile),
        check_vma=False,
    )
```

```python
import functools

import jax
import jax.numpy as jnp
from jax import lax
from jax.experimental import pallas as pl
from jax.experimental.pallas import tpu as pltpu
from jax.sharding import Mesh, PartitionSpec as P

D = 8192
FF = 14336
ZL, X, C, ZH, Y = 4, 4, 2, 2, 8
AXES = ("zl", "x", "c", "zh", "y")
DP = ("zl", "x", "c")
MP = ("zh", "y")
Q = ("zl", "x")
f32 = jnp.float32
bf16 = jnp.bfloat16
f16 = jnp.float16


def move(value, to):
    def index(zl, x, c, zh, y):
        return (((zl * X + x) * C + c) * ZH + zh) * Y + y

    pairs = [
        (index(zl, x, c, zh, y), index(*to(zl, x, c, zh, y)))
        for zl in range(ZL)
        for x in range(X)
        for c in range(C)
        for zh in range(ZH)
        for y in range(Y)
    ]
    return lax.ppermute(value, AXES, pairs)


def transpose_place(zl, x, c, zh, y):
    q, j = X * zl + x, Y * zh + y
    return j // X, j % X, c, q // Y, q % Y


def along_y(value, step):
    return move(value, lambda zl, x, c, zh, y: (zl, x, c, zh, (y + step) % Y))


def other_core(value):
    return move(value, lambda zl, x, c, zh, y: (zl, x, 1 - c, zh, y))


def other_half(value):
    return move(value, lambda zl, x, c, zh, y: (zl, x, c, 1 - zh, y))


def spread(value, axes, n):
    copies = jnp.broadcast_to(value[None], (n,) + value.shape)
    return lax.all_to_all(copies, axes, 0, 0, tiled=True)


def parts(value, n):
    out = []
    for _ in range(n - 1):
        top = lax.reduce_precision(value, 8, 7)
        out.append(top.astype(bf16))
        value = value - top
    return out + [value.astype(bf16)]


def code(value):
    largest = jnp.max(jnp.abs(value), axis=0, keepdims=True)
    scale = lax.reduce_precision(jnp.maximum(largest, 1.0) * 2.0**-14, 5, 10)
    rows = jnp.broadcast_to(scale, (16, value.shape[1]))
    return jnp.concatenate([(value / scale).astype(f16), rows.astype(f16)])


def decode(block):
    value = block[:512].astype(f32) * block[512:513].astype(f32)
    return parts(value, 2)


def near_kernel(steps, place, g_ref, *refs):
    n = len(steps)
    blocks, rest = refs[: 2 * n], refs[2 * n :]
    total, out = rest if len(rest) == 2 else (None, rest[0])
    value = None if total is None else total[...]
    for k, step in enumerate(steps):
        at = lax.rem(place[0] + (step + Y), Y)
        g = jnp.concatenate([g_ref[0, at], g_ref[1, at]], axis=0)
        for block in blocks[2 * k : 2 * k + 2]:
            term = jnp.dot(block[...], g, preferred_element_type=f32)
            value = term if value is None else value + term
    out[...] = value


def last_kernel(place, g_ref, high, low, total, out):
    rows = pl.ds(pl.multiple_of(place[0] * 256, 256), 256)
    value = total[rows, :]
    for block in (high, low):
        value += jnp.dot(block[rows, :], g_ref[...], preferred_element_type=f32)
    out[...] = value


def call(kernel, place, given, count, products):
    vmem = pl.BlockSpec(memory_space=pltpu.VMEM)
    return pl.pallas_call(
        kernel,
        out_shape=jax.ShapeDtypeStruct((count, 896), f32),
        in_specs=[pl.BlockSpec(memory_space=pltpu.SMEM)] + [vmem] * len(given),
        out_specs=vmem,
        compiler_params=pltpu.CompilerParams(vmem_limit_bytes=40 * 2**20),
        cost_estimate=pl.CostEstimate(
            flops=2 * products * 256 * count * 896,
            bytes_accessed=2**20 * products,
            transcendentals=0,
        ),
    )(place.astype(jnp.int32).reshape(1), *given)


def on_device(features, output_grads, basis, moment_one, moment_two):
    c, zh, y = lax.axis_index("c"), lax.axis_index("zh"), lax.axis_index("y")
    cotangents = lax.all_gather(output_grads, Q, axis=0, tiled=True)
    g = cotangents.reshape(ZH, Y, 128, 896)

    own = move(features, transpose_place)
    far = other_half(own)
    basis_rows = lax.all_gather(basis, "c", axis=0, tiled=True)

    partial = jnp.dot(own, basis_rows, preferred_element_type=f32)
    pieces = lax.all_to_all(partial.reshape(16, 8, 512), Q, 0, 0, tiled=True)
    summed, own, far = lax.optimization_barrier((jnp.sum(pieces, axis=0), own, far))
    both = jnp.concatenate([jnp.where(zh == 0, own, far), jnp.where(zh == 0, far, own)])
    both = both.T.astype(f32)
    coded = spread(summed, ("zh",) + Q, 32).reshape(256, 512)
    away = sum(
        lax.dot_general(
            basis_rows, p, (((1,), (1,)), ((), ())), preferred_element_type=f32
        )
        for p in parts(coded, 3)
    )
    kept = code(both - away)

    right, left = [kept], [kept]
    for _ in range(3):
        right.append(along_y(right[-1], 1))
        left.append(along_y(left[-1], -1))

    near = decode(right[0])
    for s in (1, 2):
        near += decode(right[s]) + decode(left[s])
    total = call(
        functools.partial(near_kernel, (0, -1, 1, -2, 2)), y, [g, *near], 512, 10
    )
    total, right[3], left[3] = lax.optimization_barrier((total, right[3], left[3]))
    across = [along_y(right[3][:, :128], 1), along_y(left[3][:, 128:], -1)]
    third = decode(right[3]) + decode(left[3])
    total = call(
        functools.partial(near_kernel, (-3, 3)), y, [g, *third, total], 512, 4
    )
    g_last = lax.dynamic_index_in_dim(g, lax.rem(y + 4, Y), 1, False).reshape(256, 896)
    last = [decode(half) for half in across]
    last = [jnp.concatenate(pair, axis=1) for pair in zip(*last)]
    received = other_core(call(last_kernel, 1 - c, [g_last, *last, total], 256, 2))
    projected = call(last_kernel, c, [g_last, *last, total], 256, 2) + received

    squares = jnp.sum((projected * projected).reshape(256, 7, 128), axis=(0, 1))
    squares = jnp.sum(spread(squares[None], ("x", "c", "y"), 64), axis=0)
    square_sum = jnp.sum(spread(squares, ("zh", "zl"), 8))
    mean_square = square_sum / (D * FF)
    factor = jnp.minimum(1.0, lax.rsqrt(mean_square + 1e-06))
    clipped = factor * projected
    new_one = 0.9 * moment_one + 0.1 * clipped
    new_two = 0.95 * moment_two + 0.05 * clipped * clipped
    update = (new_one / (jnp.sqrt(new_two) + 1e-08)).astype(bf16)
    return (new_one, new_two, update)


def solution(mesh):
    fine = Mesh(mesh.devices.reshape(ZL, X, C, ZH, Y), AXES)
    tile = P(DP, MP)
    return jax.shard_map(
        on_device,
        mesh=fine,
        in_specs=(tile, tile, P(DP, None), tile, tile),
        out_specs=(tile, tile, tile),
        check_vma=False,
    )
```

```python
import jax
import jax.numpy as jnp
from jax import lax
from jax.experimental import pallas as pl
from jax.experimental.pallas import tpu as pltpu
from jax.sharding import Mesh, PartitionSpec as P

D = 8192
FF = 14336
ZL, X, C, ZH, Y = 4, 4, 2, 2, 8
AXES = ("zl", "x", "c", "zh", "y")
DP = ("zl", "x", "c")
MP = ("zh", "y")
Q = ("zl", "x")
f32 = jnp.float32
bf16 = jnp.bfloat16
f16 = jnp.float16


def move(value, to):
    def index(zl, x, c, zh, y):
        return (((zl * X + x) * C + c) * ZH + zh) * Y + y

    pairs = [
        (index(zl, x, c, zh, y), index(*to(zl, x, c, zh, y)))
        for zl in range(ZL)
        for x in range(X)
        for c in range(C)
        for zh in range(ZH)
        for y in range(Y)
    ]
    return lax.ppermute(value, AXES, pairs)


def transpose_place(zl, x, c, zh, y):
    j = Y * zh + y
    return j // X, j % X, c, zl // 2, 2 * x + zl % 2


def other_core(value):
    return move(value, lambda zl, x, c, zh, y: (zl, x, 1 - c, zh, y))


def other_half(value):
    return move(value, lambda zl, x, c, zh, y: (zl, x, c, 1 - zh, y))


def spread(value, axes, n):
    copies = jnp.broadcast_to(value[None], (n,) + value.shape)
    return lax.all_to_all(copies, axes, 0, 0, tiled=True)


def parts(value, n):
    out = []
    for _ in range(n - 1):
        top = lax.reduce_precision(value, 8, 7)
        out.append(top.astype(bf16))
        value = value - top
    return out + [value.astype(bf16)]


def code(value):
    largest = jnp.max(jnp.abs(value), axis=0, keepdims=True)
    scale = lax.reduce_precision(jnp.maximum(largest * 2.0**-6, 2.0**-14), 5, 10)
    scale = jnp.where(scale * 2.0**6 < largest, scale * (1 + 2.0**-9), scale)
    scale = lax.reduce_precision(scale, 5, 10)
    share = value / (scale * 2.0**6)
    size = jnp.exp2(29.0 * jnp.abs(share) - 14.0)
    coded = jnp.where(share < 0, -size, size).astype(f16)
    return jnp.concatenate([coded, jnp.broadcast_to(scale, (16, 512)).astype(f16)])


def decode(blocks):
    coded = blocks[:, :256].astype(f32)
    share = (jnp.log2(jnp.abs(coded)) + 14.0) / 29.0
    share = jnp.where(coded < 0, -share, share)
    return parts(share * (blocks[:, 256:257].astype(f32) * 2.0**6), 2)


def grad_kernel(core, g_ref, high, low, out):
    rows = pl.ds(pl.multiple_of(core[0] * 256, 256), 256)
    value = None
    for y in range(Y):
        tokens = [g_ref[(2 * zh + y % 2) * X + y // 2] for zh in range(ZH)]
        tokens = jnp.concatenate(tokens, axis=0)
        for block in (high, low):
            term = lax.dot_general(
                block[y, :, rows],
                tokens,
                (((0,), (0,)), ((), ())),
                preferred_element_type=f32,
            )
            value = term if value is None else value + term
    out[...] = value


def call(kernel, core, g, given):
    vmem = pl.BlockSpec(memory_space=pltpu.VMEM)
    return pl.pallas_call(
        kernel,
        out_shape=jax.ShapeDtypeStruct((256, 896), f32),
        in_specs=[pl.BlockSpec(memory_space=pltpu.SMEM), vmem] + [vmem] * len(given),
        out_specs=vmem,
        compiler_params=pltpu.CompilerParams(vmem_limit_bytes=16 * 2**20),
        cost_estimate=pl.CostEstimate(
            flops=4 * 2048 * 256 * 896, bytes_accessed=8 * 2**20, transcendentals=0
        ),
    )(core.astype(jnp.int32).reshape(1), g, *given)


def on_device(features, output_grads, basis, moment_one, moment_two):
    c, zh, y = lax.axis_index("c"), lax.axis_index("zh"), lax.axis_index("y")
    g = lax.all_gather(output_grads, Q, axis=0)

    own = move(features, transpose_place)
    far = other_half(own)
    basis_rows = lax.all_gather(basis, "c", axis=0, tiled=True)

    partial = jnp.dot(own, basis_rows, preferred_element_type=f32)
    pieces = lax.all_to_all(partial.reshape(16, 8, 512), Q, 0, 0, tiled=True)
    summed, own, far = lax.optimization_barrier((jnp.sum(pieces, axis=0), own, far))
    both = jnp.concatenate([jnp.where(zh == 0, own, far), jnp.where(zh == 0, far, own)])
    coded = spread(summed, ("zh",) + Q, 32).reshape(256, 512)
    away = sum(
        lax.dot_general(
            p, basis_rows, (((1,), (1,)), ((), ())), preferred_element_type=f32
        )
        for p in parts(coded, 3)
    )
    kept = code(both.astype(f32) - away)

    blocks = lax.all_gather(kept, "y", axis=0)

    high, low = decode(blocks)

    def products(core):
        return call(grad_kernel, core, g, [high, low])

    received = other_core(products(1 - c))
    projected = products(c) + received

    squares = jnp.sum((projected * projected).reshape(256, 7, 128), axis=(0, 1))
    squares = jnp.sum(spread(squares[None], ("x", "c", "y"), 64), axis=0)
    square_sum = jnp.sum(spread(squares, ("zh", "zl"), 8))
    mean_square = square_sum / (D * FF)
    factor = jnp.minimum(1.0, lax.rsqrt(mean_square + 1e-06))
    clipped = factor * projected
    new_one = 0.9 * moment_one + 0.1 * clipped
    new_two = 0.95 * moment_two + 0.05 * clipped * clipped
    update = (new_one / (jnp.sqrt(new_two) + 1e-08)).astype(bf16)
    return (new_one, new_two, update)


def solution(mesh):
    fine = Mesh(mesh.devices.reshape(ZL, X, C, ZH, Y), AXES)
    tile = P(DP, MP)
    return jax.shard_map(
        on_device,
        mesh=fine,
        in_specs=(tile, tile, P(DP, None), tile, tile),
        out_specs=(tile, tile, tile),
        check_vma=False,
    )
```

```python
import jax
import jax.numpy as jnp
from jax import lax
from jax.experimental import pallas as pl
from jax.experimental.pallas import tpu as pltpu
from jax.sharding import Mesh, PartitionSpec as P

D = 8192
FF = 14336
ZL, X, C, ZH, Y = 4, 4, 2, 2, 8
AXES = ("zl", "x", "c", "zh", "y")
DP = ("zl", "x", "c")
MP = ("zh", "y")
Q = ("zl", "x")
f32 = jnp.float32
bf16 = jnp.bfloat16
f16 = jnp.float16


def move(value, to):
    def index(zl, x, c, zh, y):
        return (((zl * X + x) * C + c) * ZH + zh) * Y + y

    pairs = [
        (index(zl, x, c, zh, y), index(*to(zl, x, c, zh, y)))
        for zl in range(ZL)
        for x in range(X)
        for c in range(C)
        for zh in range(ZH)
        for y in range(Y)
    ]
    return lax.ppermute(value, AXES, pairs)


def transpose_place(zl, x, c, zh, y):
    j = Y * zh + y
    return j // X, j % X, c, zl // 2, 2 * x + zl % 2


def other_core(value):
    return move(value, lambda zl, x, c, zh, y: (zl, x, 1 - c, zh, y))


def other_half(value):
    return move(value, lambda zl, x, c, zh, y: (zl, x, c, 1 - zh, y))


def spread(value, axes, n):
    copies = jnp.broadcast_to(value[None], (n,) + value.shape)
    return lax.all_to_all(copies, axes, 0, 0, tiled=True)


def parts(value, n):
    out = []
    for _ in range(n - 1):
        top = lax.reduce_precision(value, 8, 7)
        out.append(top.astype(bf16))
        value = value - top
    return out + [value.astype(bf16)]


def code(value):
    largest = jnp.max(jnp.abs(value), axis=0, keepdims=True)
    scale = lax.reduce_precision(jnp.maximum(largest * 2.0**-6, 2.0**-14), 5, 10)
    scale = jnp.where(scale * 2.0**6 < largest, scale * (1 + 2.0**-9), scale)
    scale = lax.reduce_precision(scale, 5, 10)
    share = value / (scale * 2.0**6)
    size = jnp.exp2(29.0 * jnp.abs(share) - 14.0)
    coded = jnp.where(share < 0, -size, size).astype(f16)
    return jnp.concatenate([coded, jnp.broadcast_to(scale, (16, 512)).astype(f16)])


def decode(blocks):
    coded = blocks[:, :256].astype(f32)
    scale = blocks[:, 256:257].astype(f32) * (2.0**6 / 29.0)
    size = jnp.log2(jnp.abs(coded)) * scale + 14.0 * scale
    return parts(jnp.where(coded < 0, -size, size), 2)


def grad_kernel(core, g_ref, high, low, out):
    rows = pl.ds(pl.multiple_of(core[0] * 256, 256), 256)
    value = None
    for y in range(Y):
        tokens = [g_ref[y // 2, 2 * zh + y % 2] for zh in range(ZH)]
        tokens = jnp.concatenate(tokens, axis=0)
        for block in (high, low):
            term = lax.dot_general(
                block[y, :, rows],
                tokens,
                (((0,), (0,)), ((), ())),
                preferred_element_type=f32,
            )
            value = term if value is None else value + term
    out[...] = value


def call(kernel, core, g, given):
    vmem = pl.BlockSpec(memory_space=pltpu.VMEM)
    return pl.pallas_call(
        kernel,
        out_shape=jax.ShapeDtypeStruct((256, 896), f32),
        in_specs=[pl.BlockSpec(memory_space=pltpu.SMEM), vmem] + [vmem] * len(given),
        out_specs=vmem,
        compiler_params=pltpu.CompilerParams(vmem_limit_bytes=8 * 2**20),
        cost_estimate=pl.CostEstimate(
            flops=4 * 2048 * 256 * 896, bytes_accessed=8 * 2**20, transcendentals=0
        ),
    )(core.astype(jnp.int32).reshape(1), g, *given)


def on_device(features, output_grads, basis, moment_one, moment_two):
    c, zh, y = lax.axis_index("c"), lax.axis_index("zh"), lax.axis_index("y")
    own = move(features, transpose_place)
    basis_rows = lax.all_gather(basis, "c", axis=0, tiled=True)

    shard, basis_rows = lax.optimization_barrier((output_grads, basis_rows))
    column = lax.all_gather(shard, "zl", axis=0)
    column, own = lax.optimization_barrier((column, own))
    g = lax.all_gather(column, "x", axis=0)
    far = other_half(own)
    partial = jnp.dot(own, basis_rows, preferred_element_type=f32)
    pieces = lax.all_to_all(partial.reshape(16, 8, 512), Q, 0, 0, tiled=True)
    summed, own, far = lax.optimization_barrier((jnp.sum(pieces, axis=0), own, far))
    both = jnp.concatenate([jnp.where(zh == 0, own, far), jnp.where(zh == 0, far, own)])
    coded = spread(summed, ("zh",) + Q, 32).reshape(256, 512)
    away = sum(
        lax.dot_general(
            p, basis_rows, (((1,), (1,)), ((), ())), preferred_element_type=f32
        )
        for p in parts(coded, 3)
    )
    kept = code(both.astype(f32) - away)

    blocks = lax.all_gather(kept, "y", axis=0)
    blocks, g = lax.optimization_barrier((blocks, g))

    high, low = decode(blocks)

    def products(core):
        return call(grad_kernel, core, g, [high, low])

    received = other_core(products(1 - c))
    projected = products(c) + received

    squares = jnp.sum((projected * projected).reshape(256, 7, 128), axis=(0, 1))
    squares = jnp.sum(spread(squares[None], ("x", "c", "y"), 64), axis=0)
    square_sum = jnp.sum(spread(squares, ("zh", "zl"), 8))
    mean_square = square_sum / (D * FF)
    factor = jnp.minimum(1.0, lax.rsqrt(mean_square + 1e-06))
    clipped = factor * projected
    new_one = 0.9 * moment_one + 0.1 * clipped
    new_two = 0.95 * moment_two + 0.05 * clipped * clipped
    update = (new_one / (jnp.sqrt(new_two) + 1e-08)).astype(bf16)
    return (new_one, new_two, update)


def solution(mesh):
    fine = Mesh(mesh.devices.reshape(ZL, X, C, ZH, Y), AXES)
    tile = P(DP, MP)
    return jax.shard_map(
        on_device,
        mesh=fine,
        in_specs=(tile, tile, P(DP, None), tile, tile),
        out_specs=(tile, tile, tile),
        check_vma=False,
    )
```

```python
import jax
import jax.numpy as jnp
from jax import lax
from jax.experimental import pallas as pl
from jax.experimental.pallas import tpu as pltpu
from jax.sharding import Mesh, PartitionSpec as P

D = 8192
FF = 14336
ZL, X, C, ZH, Y = 4, 4, 2, 2, 8
AXES = ("zl", "x", "c", "zh", "y")
DP = ("zl", "x", "c")
MP = ("zh", "y")
Q = ("zl", "x")
f32 = jnp.float32
bf16 = jnp.bfloat16
f16 = jnp.float16


def move(value, to):
    def index(zl, x, c, zh, y):
        return (((zl * X + x) * C + c) * ZH + zh) * Y + y

    pairs = [
        (index(zl, x, c, zh, y), index(*to(zl, x, c, zh, y)))
        for zl in range(ZL)
        for x in range(X)
        for c in range(C)
        for zh in range(ZH)
        for y in range(Y)
    ]
    return lax.ppermute(value, AXES, pairs)


def transpose_place(zl, x, c, zh, y):
    return 2 * zh + y // 4, y % 4, c, zl // 2, 4 * (zl % 2) + x


def swap_x_y(zl, x, c, zh, y):
    return zl, y % 4, c, zh, 4 * (y // 4) + x


def swap_y_z(zl, x, c, zh, y):
    return 2 * zh + y // 4, x, c, zl // 2, 4 * (zl % 2) + y % 4


def other_core(value):
    return move(value, lambda zl, x, c, zh, y: (zl, x, 1 - c, zh, y))


def spread(value, axes, n):
    copies = jnp.broadcast_to(value[None], (n,) + value.shape)
    return lax.all_to_all(copies, axes, 0, 0, tiled=True)


def parts(value, n):
    out = []
    for _ in range(n - 1):
        top = lax.reduce_precision(value, 8, 7)
        out.append(top.astype(bf16))
        value = value - top
    return out + [value.astype(bf16)]


def code(value):
    largest = jnp.max(jnp.abs(value), axis=0, keepdims=True)
    scale = lax.reduce_precision(jnp.maximum(largest * 2.0**-6, 2.0**-14), 5, 10)
    scale = jnp.where(scale * 2.0**6 < largest, scale * (1 + 2.0**-9), scale)
    scale = lax.reduce_precision(scale, 5, 10)
    share = value / (scale * 2.0**6)
    size = jnp.exp2(29.0 * jnp.abs(share) - 14.0)
    coded = jnp.where(share < 0, -size, size).astype(f16)
    return jnp.concatenate([coded, jnp.broadcast_to(scale, (16, 512)).astype(f16)])


def decode(blocks):
    coded = blocks[:, :128].astype(f32)
    scale = blocks[:, 128:129].astype(f32) * (2.0**6 / 29.0)
    size = jnp.log2(jnp.abs(coded)) * scale + 14.0 * scale
    return parts(jnp.where(coded < 0, -size, size), 2)


def grad_kernel(core, g_ref, high, low, out):
    rows = pl.ds(pl.multiple_of(core[0] * 256, 256), 256)
    value = None
    for y in range(Y):
        tokens = [g_ref[y % X, 2 * zh + y // X] for zh in range(ZH)]
        tokens = jnp.concatenate(tokens, axis=0)
        for block in (high, low):
            pair = [block[ZH * y + zh, :, rows] for zh in range(ZH)]
            term = lax.dot_general(
                jnp.concatenate(pair, axis=0),
                tokens,
                (((0,), (0,)), ((), ())),
                preferred_element_type=f32,
            )
            value = term if value is None else value + term
    out[...] = value


def call(kernel, core, g, given):
    vmem = pl.BlockSpec(memory_space=pltpu.VMEM)
    return pl.pallas_call(
        kernel,
        out_shape=jax.ShapeDtypeStruct((256, 896), f32),
        in_specs=[pl.BlockSpec(memory_space=pltpu.SMEM), vmem] + [vmem] * len(given),
        out_specs=vmem,
        compiler_params=pltpu.CompilerParams(vmem_limit_bytes=8 * 2**20),
        cost_estimate=pl.CostEstimate(
            flops=4 * 2048 * 256 * 896, bytes_accessed=8 * 2**20, transcendentals=0
        ),
    )(core.astype(jnp.int32).reshape(1), g, *given)


def on_device(features, output_grads, basis, moment_one, moment_two):
    c = lax.axis_index("c")
    direct = move(features[:64], transpose_place)
    around = move(move(features[64:], swap_x_y), swap_y_z)
    own = jnp.concatenate([direct, around])
    basis_rows = lax.all_gather(basis, "c", axis=0, tiled=True)

    shard, own = lax.optimization_barrier((output_grads, own))
    column = lax.all_gather(shard, "zl", axis=0)
    partial = jnp.dot(own, basis_rows, preferred_element_type=f32)
    pieces = lax.all_to_all(partial.reshape(16, 8, 512), Q, 0, 0, tiled=True)
    column, pieces = lax.optimization_barrier((column, pieces))
    g = lax.all_gather(column, "x", axis=0)
    coded = spread(jnp.sum(pieces, axis=0), Q, 16).reshape(128, 512)
    away = sum(
        lax.dot_general(
            p, basis_rows, (((1,), (1,)), ((), ())), preferred_element_type=f32
        )
        for p in parts(coded, 3)
    )
    kept = code(own.astype(f32) - away)

    pair = lax.all_gather(kept, "zh", axis=0)
    blocks = lax.all_gather(pair, "y", axis=0).reshape(Y * ZH, 144, 512)
    blocks, g = lax.optimization_barrier((blocks, g))

    high, low = decode(blocks)

    def products(core):
        return call(grad_kernel, core, g, [high, low])

    received = other_core(products(1 - c))
    projected = products(c) + received

    squares = jnp.sum((projected * projected).reshape(256, 7, 128), axis=(0, 1))
    squares = jnp.sum(spread(squares[None], ("x", "c", "y"), 64), axis=0)
    square_sum = jnp.sum(spread(squares, ("zh", "zl"), 8))
    mean_square = square_sum / (D * FF)
    factor = jnp.minimum(1.0, lax.rsqrt(mean_square + 1e-06))
    clipped = factor * projected
    new_one = 0.9 * moment_one + 0.1 * clipped
    new_two = 0.95 * moment_two + 0.05 * clipped * clipped
    update = (new_one / (jnp.sqrt(new_two) + 1e-08)).astype(bf16)
    return (new_one, new_two, update)


def solution(mesh):
    fine = Mesh(mesh.devices.reshape(ZL, X, C, ZH, Y), AXES)
    tile = P(DP, MP)
    return jax.shard_map(
        on_device,
        mesh=fine,
        in_specs=(tile, tile, P(DP, None), tile, tile),
        out_specs=(tile, tile, tile),
        check_vma=False,
    )
```

```python
import jax
import jax.numpy as jnp
from jax import lax
from jax.experimental import pallas as pl
from jax.experimental.pallas import tpu as pltpu
from jax.sharding import Mesh, PartitionSpec as P

D = 8192
FF = 14336
ZL, X, C, ZH, Y = 4, 4, 2, 2, 8
AXES = ("zl", "x", "c", "zh", "y")
DP = ("zl", "x", "c")
MP = ("zh", "y")
Q = ("zl", "x")
f32 = jnp.float32
bf16 = jnp.bfloat16
f16 = jnp.float16


def move(value, to):
    def index(zl, x, c, zh, y):
        return (((zl * X + x) * C + c) * ZH + zh) * Y + y

    pairs = [
        (index(zl, x, c, zh, y), index(*to(zl, x, c, zh, y)))
        for zl in range(ZL)
        for x in range(X)
        for c in range(C)
        for zh in range(ZH)
        for y in range(Y)
    ]
    return lax.ppermute(value, AXES, pairs)


def transpose_place(zl, x, c, zh, y):
    return 2 * zh + y // 4, y % 4, c, zl // 2, 4 * (zl % 2) + x


def swap_x_y(zl, x, c, zh, y):
    return zl, y % 4, c, zh, 4 * (y // 4) + x


def swap_y_z(zl, x, c, zh, y):
    return 2 * zh + y // 4, x, c, zl // 2, 4 * (zl % 2) + y % 4


def other_core(value):
    return move(value, lambda zl, x, c, zh, y: (zl, x, 1 - c, zh, y))


def spread(value, axes, n):
    copies = jnp.broadcast_to(value[None], (n,) + value.shape)
    return lax.all_to_all(copies, axes, 0, 0, tiled=True)


def parts(value, n):
    out = []
    for _ in range(n - 1):
        top = lax.reduce_precision(value, 8, 7)
        out.append(top.astype(bf16))
        value = value - top
    return out + [value.astype(bf16)]


def code(value):
    largest = jnp.max(jnp.abs(value), axis=0, keepdims=True)
    scale = lax.reduce_precision(jnp.maximum(largest * 2.0**-6, 2.0**-14), 5, 10)
    scale = jnp.where(scale * 2.0**6 < largest, scale * (1 + 2.0**-9), scale)
    scale = lax.reduce_precision(scale, 5, 10)
    share = value / (scale * 2.0**6)
    size = jnp.exp2(28.0 * jnp.abs(share) - 13.0)
    coded = jnp.where(share < 0, -size, size).astype(f16)
    return jnp.concatenate([coded, jnp.broadcast_to(scale, (8, 512)).astype(f16)])


def decode(blocks):
    coded = blocks[:, :128].astype(f32)
    scale = blocks[:, 128:129].astype(f32) * (2.0**6 / 28.0)
    size = jnp.log2(jnp.abs(coded)) * scale + 13.0 * scale
    return parts(jnp.where(coded < 0, -size, size), 2)


def grad_kernel(core, g_ref, high, low, out):
    rows = pl.ds(pl.multiple_of(core[0] * 256, 256), 256)
    value = None
    for y in range(Y):
        tokens = [g_ref[y % X, 2 * zh + y // X] for zh in range(ZH)]
        tokens = jnp.concatenate(tokens, axis=0)
        for block in (high, low):
            pair = [block[ZH * y + zh, :, rows] for zh in range(ZH)]
            term = lax.dot_general(
                jnp.concatenate(pair, axis=0),
                tokens,
                (((0,), (0,)), ((), ())),
                preferred_element_type=f32,
            )
            value = term if value is None else value + term
    out[...] = value


def call(kernel, core, g, given):
    vmem = pl.BlockSpec(memory_space=pltpu.VMEM)
    return pl.pallas_call(
        kernel,
        out_shape=jax.ShapeDtypeStruct((256, 896), f32),
        in_specs=[pl.BlockSpec(memory_space=pltpu.SMEM), vmem] + [vmem] * len(given),
        out_specs=vmem,
        compiler_params=pltpu.CompilerParams(vmem_limit_bytes=8 * 2**20),
        cost_estimate=pl.CostEstimate(
            flops=4 * 2048 * 256 * 896, bytes_accessed=8 * 2**20, transcendentals=0
        ),
    )(core.astype(jnp.int32).reshape(1), g, *given)


def on_device(features, output_grads, basis, moment_one, moment_two):
    c = lax.axis_index("c")
    direct = move(features[:64], transpose_place)
    around = move(move(features[64:], swap_x_y), swap_y_z)
    own = jnp.concatenate([direct, around])
    basis_rows = lax.all_gather(basis, "c", axis=0, tiled=True)

    shard, own = lax.optimization_barrier((output_grads, own))
    column = lax.all_gather(shard, "zl", axis=0)
    partial = jnp.dot(own, basis_rows, preferred_element_type=f32)
    pieces = lax.all_to_all(partial.reshape(16, 8, 512), Q, 0, 0, tiled=True)
    column, pieces = lax.optimization_barrier((column, pieces))
    g = lax.all_gather(column, "x", axis=0)
    coded = spread(jnp.sum(pieces, axis=0), Q, 16).reshape(128, 512)
    away = sum(
        lax.dot_general(
            p, basis_rows, (((1,), (1,)), ((), ())), preferred_element_type=f32
        )
        for p in parts(coded, 3)
    )
    kept = code(own.astype(f32) - away)

    pair = lax.all_gather(kept, "zh", axis=0)
    blocks = lax.all_gather(pair, "y", axis=0).reshape(Y * ZH, 136, 512)
    blocks, g = lax.optimization_barrier((blocks, g))

    high, low = decode(blocks)

    def products(core):
        return call(grad_kernel, core, g, [high, low])

    received = other_core(products(1 - c))
    projected = products(c) + received

    squares = jnp.sum((projected * projected).reshape(256, 7, 128), axis=(0, 1))
    squares = jnp.sum(spread(squares[None], ("x", "c", "y"), 64), axis=0)
    square_sum = jnp.sum(spread(squares, ("zh", "zl"), 8))
    mean_square = square_sum / (D * FF)
    factor = jnp.minimum(1.0, lax.rsqrt(mean_square + 1e-06))
    clipped = factor * projected
    new_one = 0.9 * moment_one + 0.1 * clipped
    new_two = 0.95 * moment_two + 0.05 * clipped * clipped
    update = (new_one / (jnp.sqrt(new_two) + 1e-08)).astype(bf16)
    return (new_one, new_two, update)


def solution(mesh):
    fine = Mesh(mesh.devices.reshape(ZL, X, C, ZH, Y), AXES)
    tile = P(DP, MP)
    return jax.shard_map(
        on_device,
        mesh=fine,
        in_specs=(tile, tile, P(DP, None), tile, tile),
        out_specs=(tile, tile, tile),
        check_vma=False,
    )
```

```python
import jax
import jax.numpy as jnp
from jax import lax
from jax.experimental import pallas as pl
from jax.experimental.pallas import tpu as pltpu
from jax.sharding import Mesh, PartitionSpec as P

D = 8192
FF = 14336
ZL, X, C, ZH, Y = 4, 4, 2, 2, 8
AXES = ("zl", "x", "c", "zh", "y")
DP = ("zl", "x", "c")
MP = ("zh", "y")
Q = ("zl", "x")
f32 = jnp.float32
bf16 = jnp.bfloat16
f16 = jnp.float16


def move(value, to):
    def index(zl, x, c, zh, y):
        return (((zl * X + x) * C + c) * ZH + zh) * Y + y

    pairs = [
        (index(zl, x, c, zh, y), index(*to(zl, x, c, zh, y)))
        for zl in range(ZL)
        for x in range(X)
        for c in range(C)
        for zh in range(ZH)
        for y in range(Y)
    ]
    return lax.ppermute(value, AXES, pairs)


def transpose_place(zl, x, c, zh, y):
    return 2 * zh + y // 4, y % 4, c, zl // 2, 4 * (zl % 2) + x


def swap_x_y(zl, x, c, zh, y):
    return zl, y % 4, c, zh, 4 * (y // 4) + x


def swap_y_z(zl, x, c, zh, y):
    return 2 * zh + y // 4, x, c, zl // 2, 4 * (zl % 2) + y % 4


def other_core(value):
    return move(value, lambda zl, x, c, zh, y: (zl, x, 1 - c, zh, y))


def spread(value, axes, n):
    copies = jnp.broadcast_to(value[None], (n,) + value.shape)
    return lax.all_to_all(copies, axes, 0, 0, tiled=True)


def parts(value, n):
    out = []
    for _ in range(n - 1):
        top = lax.reduce_precision(value, 8, 7)
        out.append(top.astype(bf16))
        value = value - top
    return out + [value.astype(bf16)]


def code(value):
    largest = jnp.max(jnp.abs(value), axis=0, keepdims=True)
    scale = lax.reduce_precision(jnp.maximum(largest * 2.0**-6, 2.0**-14), 5, 10)
    scale = jnp.where(scale * 2.0**6 < largest, scale * (1 + 2.0**-9), scale)
    scale = lax.reduce_precision(scale, 5, 10)
    share = value / (scale * 2.0**6)
    size = jnp.exp2(28.0 * jnp.abs(share) - 13.0)
    coded = jnp.where(share < 0, -size, size).astype(f16)
    return jnp.concatenate([coded, jnp.broadcast_to(scale, (8, 512)).astype(f16)])


def decode(blocks):
    coded = blocks[:, :128].astype(f32)
    scale = blocks[:, 128:129].astype(f32) * (2.0**6 / 28.0)
    size = jnp.log2(jnp.abs(coded)) * scale + 13.0 * scale
    return parts(jnp.where(coded < 0, -size, size), 2)


def grad_kernel(core, g_ref, high, low, out):
    rows = pl.ds(pl.multiple_of(core[0] * 256, 256), 256)
    tokens = [g_ref[y % X, 2 * zh + y // X] for y in range(Y) for zh in range(ZH)]
    tokens = jnp.concatenate(tokens, axis=0)
    terms = [
        lax.dot_general(
            block[:, :, rows].reshape(2048, 256),
            tokens,
            (((0,), (0,)), ((), ())),
            preferred_element_type=f32,
        )
        for block in (high, low)
    ]
    out[...] = terms[0] + terms[1]


def call(kernel, core, g, given):
    vmem = pl.BlockSpec(memory_space=pltpu.VMEM)
    return pl.pallas_call(
        kernel,
        out_shape=jax.ShapeDtypeStruct((256, 896), f32),
        in_specs=[pl.BlockSpec(memory_space=pltpu.SMEM), vmem] + [vmem] * len(given),
        out_specs=vmem,
        compiler_params=pltpu.CompilerParams(vmem_limit_bytes=8 * 2**20),
        cost_estimate=pl.CostEstimate(
            flops=4 * 2048 * 256 * 896, bytes_accessed=8 * 2**20, transcendentals=0
        ),
    )(core.astype(jnp.int32).reshape(1), g, *given)


def on_device(features, output_grads, basis, moment_one, moment_two):
    c = lax.axis_index("c")
    direct = move(features[:64], transpose_place)
    around = move(move(features[64:], swap_x_y), swap_y_z)
    own = jnp.concatenate([direct, around])
    basis_rows = lax.all_gather(basis, "c", axis=0, tiled=True)

    shard, own = lax.optimization_barrier((output_grads, own))
    column = lax.all_gather(shard, "zl", axis=0)
    partial = jnp.dot(own, basis_rows, preferred_element_type=f32)
    pieces = lax.all_to_all(partial.reshape(16, 8, 512), Q, 0, 0, tiled=True)
    column, pieces = lax.optimization_barrier((column, pieces))
    g = lax.all_gather(column, "x", axis=0)
    coded = spread(jnp.sum(pieces, axis=0), Q, 16).reshape(128, 512)
    away = sum(
        lax.dot_general(
            p, basis_rows, (((1,), (1,)), ((), ())), preferred_element_type=f32
        )
        for p in parts(coded, 3)
    )
    kept = code(own.astype(f32) - away)

    pair = lax.all_gather(kept, "zh", axis=0)
    blocks = lax.all_gather(pair, "y", axis=0).reshape(Y * ZH, 136, 512)
    blocks, g = lax.optimization_barrier((blocks, g))

    high, low = decode(blocks)

    def products(core):
        return call(grad_kernel, core, g, [high, low])

    received = other_core(products(1 - c))
    projected = products(c) + received

    squares = jnp.sum((projected * projected).reshape(256, 7, 128), axis=(0, 1))
    squares = jnp.sum(spread(squares[None], ("x", "c", "y"), 64), axis=0)
    square_sum = jnp.sum(spread(squares, ("zh", "zl"), 8))
    mean_square = square_sum / (D * FF)
    factor = jnp.minimum(1.0, lax.rsqrt(mean_square + 1e-06))
    clipped = factor * projected
    new_one = 0.9 * moment_one + 0.1 * clipped
    new_two = 0.95 * moment_two + 0.05 * clipped * clipped
    update = (new_one / (jnp.sqrt(new_two) + 1e-08)).astype(bf16)
    return (new_one, new_two, update)


def solution(mesh):
    fine = Mesh(mesh.devices.reshape(ZL, X, C, ZH, Y), AXES)
    tile = P(DP, MP)
    return jax.shard_map(
        on_device,
        mesh=fine,
        in_specs=(tile, tile, P(DP, None), tile, tile),
        out_specs=(tile, tile, tile),
        check_vma=False,
    )
```
